128 devices in a mesh: seq: 32 (over y, x_lo, z), batch: 4 (over x_hi, core).
Axes of the slice: x: 4 (x_hi: 2, x_lo: 2; x = x_hi * 2 + x_lo), y: 4, z: 4, core: 2. Of those that a mesh axis runs over, the one named last changes fastest.
Arguments:
- stream: bfloat16 [229376, 1280], P(('batch', 'seq')), parts along dimension 0, may hold values from -6 to 6
- bases: int32 [229376], P(('batch', 'seq')), parts along dimension 0, may hold values from 0 to 4
- input_weight: bfloat16 [2, 1280, 640], replicated, may hold values from -0.15625 to 0.15625
- kernel: bfloat16 [2, 5, 640, 640], replicated, may hold values from -0.109375 to 0.109375
- output_weight: bfloat16 [2, 640, 1280], replicated, may hold values from -0.25 to 0.25
Outputs:
- result: bfloat16 [229376, 1280], P(('batch', 'seq')), parts along dimension 0
The draws below stay inside these ranges and needn't reach their ends.
There are 4 independent parts, one for each index of `batch`. The reference program is written for one: setup_inputs(seed, part) draws one part's arguments, and reference() takes and returns one part's arrays. A program takes and returns all parts, laid end to end along the dimension named above; an argument that names none is the same for every part. Nothing has to cross between parts.
Inputs may be any that keep to these rules, and one draw needn't show every extreme that they name: `bases`: id 4 marks an unknown base, 0 to 3 the four nucleotides.
All inputs are finite; a program needn't handle non-finite values.
Results may differ from the reference program's by a relative error of at most 0.0085.
Values may be sent and summed in bfloat16 or wider, within the bound.
A program may use at most 128 MiB of HBM per device.

```python
import jax
import jax.numpy as jnp
from jax import lax

D = 1280
H = 640
TAPS = 5
BLOCKS = 2
SEQ_LEN = 57344
NEAR_DILATION = 896
FAR_DILATION = 14336


def plant(entries, key, least, high):
    shape = entries.shape
    spot = [jax.random.randint(jax.random.fold_in(key, axis), (), 0, shape[axis]) for axis in range(len(shape))]
    entries = entries.at[tuple(spot)].set(least)
    longest = shape.index(max(shape))
    spot[longest] = (spot[longest] + 1) % shape[longest]
    return entries.at[tuple(spot)].set(high)


def block_levels(stream_key, extent, cuts, least, top_value):
    def one(dim, parts):
        steps = jax.random.uniform(jax.random.fold_in(jax.random.fold_in(stream_key, 6), dim), (parts,), jnp.float32, least / len(cuts), top_value / len(cuts))
        return jnp.repeat(jnp.exp(steps), extent[dim] // parts).reshape((-1,) + (1,) * (len(extent) - dim - 1))

    gain = one(*cuts[0])
    for cut in cuts[1:]:
        gain = gain * one(*cut)
    return gain


def normal_values(own_key, extent, width, most, cuts=(), dtype=jnp.bfloat16):
    factor_of = block_levels(own_key, extent, cuts, -0.22, 0.18) if cuts else 1.0
    drawn = jax.random.normal(own_key, extent, jnp.float32) * width * factor_of
    return jnp.minimum(jnp.maximum(drawn, -most), most).astype(dtype)


def setup_inputs(seed: int = 0, part: int = 0) -> dict:
    arg_keys = jax.random.split(jax.random.key(seed), 6)
    part_keys = jax.random.split(jax.random.fold_in(arg_keys[5], part), 6)
    stream = normal_values(part_keys[0], (SEQ_LEN, D), 1.0, 6.0, ((0, 32),))
    bases = plant(jax.random.randint(part_keys[1], (SEQ_LEN,), 0, 5), jax.random.fold_in(part_keys[1], 1), 0, 4).astype(jnp.int32)
    input_weight = normal_values(arg_keys[2], (BLOCKS, D, H), D ** -0.5, 0.15625)
    kernel = normal_values(arg_keys[3], (BLOCKS, TAPS, H, H), (TAPS * H) ** -0.5, 0.109375)
    output_weight = normal_values(arg_keys[4], (BLOCKS, H, D), H ** -0.5, 0.25)
    return {"stream": stream, "bases": bases, "input_weight": input_weight, "kernel": kernel, "output_weight": output_weight}


def normed(values):
    centre = values - lax.optimization_barrier(jnp.mean(values, axis=-1, keepdims=True))
    spread = lax.optimization_barrier(jnp.mean(centre * centre, axis=-1, keepdims=True))
    return centre * lax.rsqrt(spread + 1e-05)

def dilated_residual_block(residual_stream, known_base_mask, proj_in, taps_weight, proj_out, dilation):
    total = residual_stream.shape[0]
    normed_in = jax.nn.gelu(normed(residual_stream)).astype(jnp.bfloat16)
    lowered = jnp.dot(normed_in, proj_in, preferred_element_type=jnp.float32)
    inner = (jax.nn.gelu(normed(lowered)) * known_base_mask).astype(jnp.bfloat16)
    padded = jnp.pad(inner, ((2 * dilation, 2 * dilation), (0, 0)))
    mixed = jnp.zeros((total, inner.shape[1]), jnp.float32)
    for kernel_tap_index in range(TAPS):
        start_offset = kernel_tap_index * dilation
        mixed = mixed + jnp.dot(padded[start_offset:start_offset + total], taps_weight[kernel_tap_index], preferred_element_type=jnp.float32)
    activated = jax.nn.gelu(normed(mixed)).astype(jnp.bfloat16)
    return residual_stream + jnp.dot(activated, proj_out, preferred_element_type=jnp.float32)

def reference(stream, bases, input_weight, kernel, output_weight):
    known_base_mask = (bases != 4).astype(jnp.float32)[:, None]
    residual_stream = stream.astype(jnp.float32)
    residual_stream = dilated_residual_block(residual_stream, known_base_mask, input_weight[0], kernel[0], output_weight[0], NEAR_DILATION)
    residual_stream = dilated_residual_block(residual_stream, known_base_mask, input_weight[1], kernel[1], output_weight[1], FAR_DILATION)
    return residual_stream.astype(jnp.bfloat16)
```

```python
import functools

import jax
import jax.numpy as jnp
from jax import lax
from jax.experimental import pallas as pl
from jax.experimental.pallas import tpu as pltpu
from jax.sharding import PartitionSpec as P

D, H, TAPS = 1280, 640, 5
PITCH = 896
Q = 32
N = 4 * Q
CHUNKS = PITCH // N
ROWS = 2 * N
HALF = ROWS // 2
BF, F32 = jnp.bfloat16, jnp.float32


def gelu_of_norm(v, mask=None):
    centre = v - jnp.mean(v, axis=-1, keepdims=True)
    scale = lax.rsqrt(jnp.mean(centre * centre, axis=-1, keepdims=True) + 1e-05)
    if mask is not None:
        scale = scale * mask
    u = centre * scale
    half = 0.5 * u
    bent = u * (0.7978845608028654 + 0.035677408136300125 * (u * u))
    return (half + half * jnp.tanh(bent)).astype(BF)


def dot(a, b):
    return jnp.dot(a, b, preferred_element_type=F32)


def kernel(
    x_hbm, present, win_hbm, kern_hbm, wout_hbm, out_hbm,
    sbuf, resid, win, kern, wout,
    snd1, x1, act1, a1, i2, x2, act2, af,
    load_sem, w_sem, out_sem,
    a_s, a_r, h_s, h_r, b_s, b_r, y_s, y_r,
):
    s = lax.axis_index("seq")
    y, g, z = s // 8, s // 4, s % 4
    low = y % 2
    upper = y // 2
    own_v = low + upper - 2 * low * upper
    keep = (1 - own_v) * HALF
    give = own_v * HALF
    partner = s + 8 - 16 * low
    cross = (3 - y) * 8 + s % 8
    base = s - z

    def remote(src, dst, send, recv, dev):
        return pltpu.make_async_remote_copy(
            src_ref=src, dst_ref=dst, send_sem=send, recv_sem=recv,
            device_id={"seq": dev}, device_id_type=pl.DeviceIdType.MESH,
        )

    def rows(start, size):
        return pl.ds(pl.multiple_of(start, 16), size)

    def peer(k):
        return (z + k) % 4

    def gather(c, k):
        p = peer(k)
        return remote(
            snd1.at[c, rows(p * 2 * Q, 2 * Q)], x1.at[c, rows((2 + 2 * z) * Q, 2 * Q)],
            a_s.at[c, k - 1], a_r.at[c, k - 1], base + p,
        )

    def back(c, k):
        p = peer(k)
        return remote(
            act1.at[c, rows(p * 2 * Q, 2 * Q)], a1.at[c, rows(z * 2 * Q, 2 * Q)],
            b_s.at[c, k - 1], b_r.at[c, k - 1], base + p,
        )

    def halo_up(c):
        return remote(
            x1.at[c, pl.ds(8 * Q, 2 * Q)], x1.at[c, pl.ds(0, 2 * Q)],
            h_s.at[c, 0], h_r.at[c, 0], s + 4,
        )

    def halo_down(c):
        return remote(
            x1.at[c, pl.ds(2 * Q, 2 * Q)], x1.at[c, pl.ds(10 * Q, 2 * Q)],
            h_s.at[c, 1], h_r.at[c, 1], s - 4,
        )

    def to_partner(c):
        return remote(
            i2.at[c, rows(give, HALF)], x2.at[c, rows((y + 1) * HALF, HALF)],
            y_s.at[c, 0], y_r.at[c, 0], partner,
        )

    def to_cross(c):
        return remote(
            i2.at[c, rows(keep, HALF)], x2.at[c, rows((y + 1) * HALF, HALF)],
            y_s.at[c, 1], y_r.at[c, 1], cross,
        )

    def relay(c):
        slot = y + 2 - 2 * low
        part = x2.at[c, rows(slot * HALF, HALF)]
        return remote(part, part, y_s.at[c, 2], y_r.at[c, 2], cross)

    def to_home(c):
        return remote(
            act2.at[c, rows((1 - low) * HALF, HALF)], af.at[c, rows((1 - own_v) * HALF, HALF)],
            y_s.at[c, 3], y_r.at[c, 3], partner,
        )

    def load(c, h):
        return pltpu.make_async_copy(x_hbm.at[h, pl.ds(4 * c, 4)], sbuf.at[c, :, h], load_sem.at[c, h])

    def store(c, h):
        return pltpu.make_async_copy(sbuf.at[c, :, h], out_hbm.at[h, pl.ds(4 * c, 4)], out_sem.at[c, h])

    weights = {
        "in0": pltpu.make_async_copy(win_hbm.at[0], win.at[0], w_sem.at[0]),
        "k0": pltpu.make_async_copy(kern_hbm.at[0], kern.at[0], w_sem.at[1]),
        "out0": pltpu.make_async_copy(wout_hbm.at[0], wout.at[0], w_sem.at[2]),
        "in1": pltpu.make_async_copy(win_hbm.at[1], win.at[1], w_sem.at[3]),
        "k1": pltpu.make_async_copy(kern_hbm.at[1], kern.at[1], w_sem.at[4]),
        "out1": pltpu.make_async_copy(wout_hbm.at[1], wout.at[1], w_sem.at[5]),
    }

    def first(c, *names):
        @pl.when(c == 0)
        def _():
            for name in names:
                weights[name].wait()

    def lower_first(c):
        load(c, 0).wait()
        load(c, 1).wait()
        first(c, "in0")
        v = sbuf[c].reshape(ROWS, D).astype(F32)
        lowered = dot(gelu_of_norm(v), win[0])
        snd1[c] = gelu_of_norm(lowered, present[c])

        @pl.when(c == 0)
        def _():
            pl.semaphore_wait(barrier, 5 + (g + 6) // 7 + (13 - g) // 7)

        for k in (1, 2, 3):
            gather(c, k).start()
        x1[c, rows((2 + 2 * z) * Q, 2 * Q)] = snd1[c, rows(z * 2 * Q, 2 * Q)]

    def send_halo(c):
        for k in (1, 2, 3):
            gather(c, k).wait_recv()

        @pl.when(g < 7)
        def _():
            halo_up(c).start()

        @pl.when(g > 0)
        def _():
            halo_down(c).start()

    def near(c):
        first(c, "k0")

        @pl.when(g > 0)
        def _():
            halo_up(c).wait_recv()

        @pl.when(g < 7)
        def _():
            halo_down(c).wait_recv()

        wide = jnp.concatenate([x1[c, pl.ds(k * Q, 8 * Q)] for k in range(TAPS)], axis=1)
        act1[c] = gelu_of_norm(dot(wide, kern[0]))
        for k in (1, 2, 3):
            back(c, k).start()
        a1[c, rows(z * 2 * Q, 2 * Q)] = act1[c, rows(z * 2 * Q, 2 * Q)]

    def middle(c):
        first(c, "out0", "in1")
        for k in (1, 2, 3):
            back(c, k).wait_recv()
        resid[c] = sbuf[c].reshape(ROWS, D).astype(F32) + dot(a1[c], wout[0])
        lowered = dot(gelu_of_norm(resid[c]), win[1])
        i2[c] = gelu_of_norm(lowered, present[c])
        to_partner(c).start()
        to_cross(c).start()
        x2[c, rows((y + 1) * HALF, HALF)] = i2[c, rows(keep, HALF)]

    def pass_on(c):
        to_partner(c).wait_recv()
        relay(c).start()

    def far(c):
        first(c, "k1")
        to_cross(c).wait_recv()
        relay(c).wait_recv()
        wide = jnp.concatenate(
            [x2[c, rows((upper + k) * HALF, ROWS)] for k in range(4)], axis=1
        )
        act2[c] = gelu_of_norm(dot(wide, kern[1, rows((1 - upper) * H, 4 * H)]))
        to_home(c).start()
        af[c, rows(keep, HALF)] = act2[c, rows(low * HALF, HALF)]

    def finish(c):
        first(c, "out1")
        to_home(c).wait_recv()
        result = resid[c] + dot(af[c], wout[1])
        sbuf[c] = result.astype(BF).reshape(4, 2, Q, D)
        store(c, 0).start()
        store(c, 1).start()

    barrier = pltpu.get_barrier_semaphore()

    def greet(dev):
        pl.semaphore_signal(barrier, inc=1, device_id={"seq": dev}, device_id_type=pl.DeviceIdType.MESH)

    for k in (1, 2, 3):
        greet(base + peer(k))
    greet(partner)
    greet(cross)
    pl.when(g < 7)(lambda: greet(s + 4))
    pl.when(g > 0)(lambda: greet(s - 4))

    load(0, 0).start()
    load(0, 1).start()
    weights["in0"].start()
    for c in range(1, CHUNKS):
        load(c, 0).start()
        load(c, 1).start()
        if c == 1:
            weights["k0"].start()
        if c == 2:
            weights["out0"].start()
            weights["in1"].start()
    weights["k1"].start()
    weights["out1"].start()

    def clear(c, carry):
        x2[c, pl.ds(0, HALF)] = jnp.zeros((HALF, H), BF)
        x2[c, pl.ds(5 * HALF, HALF)] = jnp.zeros((HALF, H), BF)

        @pl.when(g == 0)
        def _():
            x1[c, pl.ds(0, 2 * Q)] = jnp.zeros((2 * Q, H), BF)

        @pl.when(g == 7)
        def _():
            x1[c, pl.ds(10 * Q, 2 * Q)] = jnp.zeros((2 * Q, H), BF)

        return carry

    lax.fori_loop(0, CHUNKS, clear, 0)

    def at(c, stage):
        @pl.when(jnp.logical_and(c >= 0, c < CHUNKS))
        def _():
            stage(c)

    def step(t, carry):
        at(t, lower_first)
        at(t - 1, near)
        at(t - 3, far)
        at(t - 2, pass_on)
        at(t, send_halo)
        at(t - 4, finish)
        at(t - 1, middle)
        return carry

    lax.fori_loop(0, CHUNKS + 4, step, 0)

    def drain(c, carry):
        for k in (1, 2, 3):
            gather(c, k).wait_send()
            back(c, k).wait_send()
        pl.when(g < 7)(lambda: halo_up(c).wait_send())
        pl.when(g > 0)(lambda: halo_down(c).wait_send())
        to_partner(c).wait_send()
        to_cross(c).wait_send()
        relay(c).wait_send()
        to_home(c).wait_send()
        store(c, 0).wait()
        store(c, 1).wait()
        return carry

    lax.fori_loop(0, CHUNKS, drain, 0)


def body(stream, bases, input_weight, kernel_weight, output_weight):
    present = (bases != 4).astype(F32).reshape(2, CHUNKS, 4, Q)
    present = present.transpose(1, 2, 0, 3).reshape(CHUNKS, ROWS, 1)
    hbm = pl.BlockSpec(memory_space=pl.ANY)
    vmem = pl.BlockSpec(memory_space=pltpu.VMEM)
    dma = pltpu.SemaphoreType.DMA
    per_chunk = pltpu.VMEM((CHUNKS, ROWS, H), BF)
    result = pl.pallas_call(
        kernel,
        out_shape=jax.ShapeDtypeStruct((2, 4 * CHUNKS, Q, D), BF),
        in_specs=[hbm, vmem, hbm, hbm, hbm],
        out_specs=hbm,
        scratch_shapes=[
            pltpu.VMEM((CHUNKS, 4, 2, Q, D), BF),
            pltpu.VMEM((CHUNKS, ROWS, D), F32),
            pltpu.VMEM((2, D, H), BF),
            pltpu.VMEM((2, TAPS * H, H), BF),
            pltpu.VMEM((2, H, D), BF),
            per_chunk,
            pltpu.VMEM((CHUNKS, 12 * Q, H), BF),
            per_chunk,
            per_chunk,
            per_chunk,
            pltpu.VMEM((CHUNKS, 6 * HALF, H), BF),
            per_chunk,
            per_chunk,
            dma((CHUNKS, 2)),
            dma((6,)),
            dma((CHUNKS, 2)),
            dma((CHUNKS, 3)),
            dma((CHUNKS, 3)),
            dma((CHUNKS, 2)),
            dma((CHUNKS, 2)),
            dma((CHUNKS, 3)),
            dma((CHUNKS, 3)),
            dma((CHUNKS, 4)),
            dma((CHUNKS, 4)),
        ],
        compiler_params=pltpu.CompilerParams(
            collective_id=0, has_side_effects=True, vmem_limit_bytes=62 * 2**20
        ),
    )(
        stream.reshape(2, 4 * CHUNKS, Q, D),
        present,
        input_weight,
        kernel_weight.reshape(2, TAPS * H, H),
        output_weight,
    )
    return result.reshape(2 * PITCH, D)


def solution(mesh):
    return jax.shard_map(
        body,
        mesh=mesh,
        in_specs=(P(("batch", "seq"), None), P(("batch", "seq")), P(), P(), P()),
        out_specs=P(("batch", "seq"), None),
        check_vma=False,
    )
```

```python
import jax
import jax.numpy as jnp
from jax import lax
from jax.experimental import pallas as pl
from jax.experimental.pallas import tpu as pltpu
from jax.sharding import PartitionSpec as P

D, H, TAPS = 1280, 640, 5
PITCH = 896
FRONT, BIG, BACK = 1, 6, 1
CHUNKS = FRONT + BIG + BACK
BF, F32 = jnp.bfloat16, jnp.float32
VMEM_LIMIT = 54 * 2**20


def gelu_of_norm(v, mask=None):
    centre = v - jnp.mean(v, axis=-1, keepdims=True)
    scale = lax.rsqrt(jnp.mean(centre * centre, axis=-1, keepdims=True) + 1e-05)
    if mask is not None:
        scale = scale * mask
    u = centre * scale
    half = 0.5 * u
    bent = u * (0.7978845608028654 + 0.035677408136300125 * (u * u))
    return (half + half * jnp.tanh(bent)).astype(BF)


def dot(a, b):
    return jnp.dot(a, b, preferred_element_type=F32)


class Chunks:
    def __init__(self, q, count, refs):
        self.q, self.count = q, count
        self.rows, self.half = 8 * q, 4 * q
        if refs is None:
            return
        (
            self.sbuf, self.resid, self.pres, self.s1, self.x1, self.s2, self.a1, self.x2,
            self.load_sem, self.out_sem, self.a_s, self.a_r, self.h_s, self.h_r,
            self.b_s, self.b_r, self.y_s, self.y_r,
        ) = refs

    def scratch(self):
        q, n = self.q, self.count
        dma = pltpu.SemaphoreType.DMA
        plain = pltpu.VMEM((n, self.rows, H), BF)
        return [
            pltpu.VMEM((n, 4, 2, q, D), BF),
            pltpu.VMEM((n, self.rows, D), F32),
            pltpu.VMEM((n, 4, 2, q, 1), F32),
            plain,
            pltpu.VMEM((n, 12 * q, H), BF),
            plain,
            plain,
            pltpu.VMEM((n, 6 * self.half, H), BF),
            dma((n, 2, 4)),
            dma((n, 2, 4)),
            dma((n, 3)),
            dma((n, 3)),
            dma((n, 2)),
            dma((n, 2)),
            dma((n, 3)),
            dma((n, 3)),
            dma((n, 4)),
            dma((n, 4)),
        ]


SETS = ((16, FRONT + BACK), (32, BIG))
FIELDS = 18


def rows(start, size):
    return pl.ds(pl.multiple_of(start, 16), size)


def kernel(x_hbm, bases, win_hbm, kern_hbm, wout_hbm, out_hbm, win, kern, wout, w_sem, *refs):
    small = Chunks(*SETS[0], refs[:FIELDS])
    big = Chunks(*SETS[1], refs[FIELDS:])
    s = lax.axis_index("seq")
    y, g, z = s // 8, s // 4, s % 4
    low = y % 2
    upper = y // 2
    own_v = low + upper - 2 * low * upper
    partner = s + 8 - 16 * low
    cross = (3 - y) * 8 + s % 8
    base = s - z

    def remote(src, dst, send, recv, dev):
        return pltpu.make_async_remote_copy(
            src_ref=src, dst_ref=dst, send_sem=send, recv_sem=recv,
            device_id={"seq": dev}, device_id_type=pl.DeviceIdType.MESH,
        )

    def peer(k):
        return (z + k) % 4

    def gather(m, c, k):
        p, n = peer(k), 2 * m.q
        return remote(
            m.s1.at[c, rows(p * n, n)], m.x1.at[c, rows((1 + z) * n, n)],
            m.a_s.at[c, k - 1], m.a_r.at[c, k - 1], base + p,
        )

    def back(m, c, k):
        p, n = peer(k), 2 * m.q
        return remote(
            m.s2.at[c, rows(p * n, n)], m.a1.at[c, rows(z * n, n)],
            m.b_s.at[c, k - 1], m.b_r.at[c, k - 1], base + p,
        )

    def halo_up(m, c):
        n = 2 * m.q
        return remote(
            m.x1.at[c, pl.ds(4 * n, n)], m.x1.at[c, pl.ds(0, n)],
            m.h_s.at[c, 0], m.h_r.at[c, 0], s + 4,
        )

    def halo_down(m, c):
        n = 2 * m.q
        return remote(
            m.x1.at[c, pl.ds(n, n)], m.x1.at[c, pl.ds(5 * n, n)],
            m.h_s.at[c, 1], m.h_r.at[c, 1], s - 4,
        )

    def to_partner(m, c):
        return remote(
            m.s2.at[c, rows(own_v * m.half, m.half)], m.x2.at[c, rows((y + 1) * m.half, m.half)],
            m.y_s.at[c, 0], m.y_r.at[c, 0], partner,
        )

    def to_cross(m, c):
        return remote(
            m.s2.at[c, rows((1 - own_v) * m.half, m.half)], m.x2.at[c, rows((y + 1) * m.half, m.half)],
            m.y_s.at[c, 1], m.y_r.at[c, 1], cross,
        )

    def relay(m, c):
        part = m.x2.at[c, rows((y + 2 - 2 * low) * m.half, m.half)]
        return remote(part, part, m.y_s.at[c, 2], m.y_r.at[c, 2], cross)

    def to_home(m, c):
        return remote(
            m.s1.at[c, rows((1 - low) * m.half, m.half)], m.a1.at[c, rows((1 - own_v) * m.half, m.half)],
            m.y_s.at[c, 3], m.y_r.at[c, 3], partner,
        )

    def moves(m, c, hbm, sem, store):
        copies = []
        for h in range(2):
            if m is big:
                there, here = hbm.at[h, pl.ds(2 * FRONT + 4 * c, 4)], m.sbuf.at[c, :, h]
                pairs = [(there, here)]
            else:
                first = c * 2 if c < FRONT else 2 * c + 4 * BIG
                pairs = [
                    (hbm.at[h, first + i // 2, pl.ds(16 * (i % 2), 16)], m.sbuf.at[c, i, h])
                    for i in range(4)
                ]
            for i, (there, here) in enumerate(pairs):
                ends = (here, there) if store else (there, here)
                copies.append(pltpu.make_async_copy(*ends, sem.at[c, h, i]))
        return copies

    def loads(m, c):
        return moves(m, c, x_hbm, m.load_sem, False)

    def stores(m, c):
        return moves(m, c, out_hbm, m.out_sem, True)

    weights = {
        "in0": pltpu.make_async_copy(win_hbm.at[0], win.at[0], w_sem.at[0]),
        "k0": pltpu.make_async_copy(kern_hbm.at[0], kern.at[0], w_sem.at[1]),
        "out0": pltpu.make_async_copy(wout_hbm.at[0], wout.at[0], w_sem.at[2]),
        "in1": pltpu.make_async_copy(win_hbm.at[1], win.at[1], w_sem.at[3]),
        "k1": pltpu.make_async_copy(kern_hbm.at[1], kern.at[1], w_sem.at[4]),
        "out1": pltpu.make_async_copy(wout_hbm.at[1], wout.at[1], w_sem.at[5]),
    }

    def first(m, c, *names):
        if m is small and c == 0:
            for name in names:
                weights[name].wait()

    def lower_first(m, c):
        for copy in loads(m, c):
            copy.wait()
        first(m, c, "in0")
        v = m.sbuf[c].reshape(m.rows, D).astype(F32)
        lowered = dot(gelu_of_norm(v), win[0])
        m.s1[c] = gelu_of_norm(lowered, m.pres[c].reshape(m.rows, 1))
        if m is small and c == 0:
            pl.semaphore_wait(barrier, 5 + (g + 6) // 7 + (13 - g) // 7)
        for k in (2, 1, 3):
            gather(m, c, k).start()
        n = 2 * m.q
        m.x1[c, rows((1 + z) * n, n)] = m.s1[c, rows(z * n, n)]

    def send_halo(m, c):
        for k in (1, 2, 3):
            gather(m, c, k).wait_recv()
        pl.when(g < 7)(lambda: halo_up(m, c).start())
        pl.when(g > 0)(lambda: halo_down(m, c).start())

    def near(m, c):
        first(m, c, "k0")
        pl.when(g > 0)(lambda: halo_up(m, c).wait_recv())
        pl.when(g < 7)(lambda: halo_down(m, c).wait_recv())
        wide = jnp.concatenate([m.x1[c, pl.ds(k * m.q, 8 * m.q)] for k in range(TAPS)], axis=1)
        m.s2[c] = gelu_of_norm(dot(wide, kern[0]))
        for k in (2, 1, 3):
            back(m, c, k).start()
        n = 2 * m.q
        m.a1[c, rows(z * n, n)] = m.s2[c, rows(z * n, n)]

    def middle(m, c):
        first(m, c, "out0", "in1")
        for k in (1, 2, 3):
            back(m, c, k).wait_recv()
        m.resid[c] = m.sbuf[c].reshape(m.rows, D).astype(F32) + dot(m.a1[c], wout[0])
        lowered = dot(gelu_of_norm(m.resid[c]), win[1])
        for k in (1, 2, 3):
            back(m, c, k).wait_send()
        m.s2[c] = gelu_of_norm(lowered, m.pres[c].reshape(m.rows, 1))
        to_partner(m, c).start()
        to_cross(m, c).start()
        m.x2[c, rows((y + 1) * m.half, m.half)] = m.s2[c, rows((1 - own_v) * m.half, m.half)]

    def pass_on(m, c):
        to_partner(m, c).wait_recv()
        relay(m, c).start()

    def far(m, c):
        first(m, c, "k1")
        to_cross(m, c).wait_recv()
        relay(m, c).wait_recv()
        for k in (1, 2, 3):
            gather(m, c, k).wait_send()
        wide = jnp.concatenate(
            [m.x2[c, rows((upper + k) * m.half, m.rows)] for k in range(4)], axis=1
        )
        m.s1[c] = gelu_of_norm(dot(wide, kern[1, rows((1 - upper) * H, 4 * H)]))
        to_home(m, c).start()
        m.a1[c, rows((1 - own_v) * m.half, m.half)] = m.s1[c, rows(low * m.half, m.half)]

    def finish(m, c):
        first(m, c, "out1")
        to_home(m, c).wait_recv()
        result = m.resid[c] + dot(m.a1[c], wout[1])
        m.sbuf[c] = result.astype(BF).reshape(4, 2, m.q, D)
        for copy in stores(m, c):
            copy.start()

    barrier = pltpu.get_barrier_semaphore()

    def greet(dev):
        pl.semaphore_signal(barrier, inc=1, device_id={"seq": dev}, device_id_type=pl.DeviceIdType.MESH)

    for k in (1, 2, 3):
        greet(base + peer(k))
    greet(partner)
    greet(cross)
    pl.when(g < 7)(lambda: greet(s + 4))
    pl.when(g > 0)(lambda: greet(s - 4))

    order = [(small, c) for c in range(FRONT)]
    order += [(big, c) for c in range(BIG)]
    order += [(small, c) for c in range(FRONT, FRONT + BACK)]
    for i, (m, c) in enumerate(order):
        for copy in loads(m, c):
            copy.start()
        if i == 0:
            weights["in0"].start()
        if i == 1:
            weights["k0"].start()
        if i == 2:
            weights["out0"].start()
            weights["in1"].start()
    weights["k1"].start()
    weights["out1"].start()

    known = (bases[...] != 4).astype(F32).T
    for c, (m, i) in enumerate(order):
        n = 4 * m.q
        start = 64 * c if c <= FRONT else 64 * FRONT + 128 * (c - FRONT)
        if c > FRONT + BIG:
            start = 64 * (c - BIG) + 128 * BIG
        for h in range(2):
            for j in range(4):
                at = start + j * m.q
                col = h * 7 + at // 128
                m.pres[i, j, h] = known[at % 128 : at % 128 + m.q, col : col + 1]

    for m in (small, big):

        def clear(c, carry):
            m.x2[c, pl.ds(0, m.half)] = jnp.zeros((m.half, H), BF)
            m.x2[c, pl.ds(5 * m.half, m.half)] = jnp.zeros((m.half, H), BF)

            @pl.when(g == 0)
            def _():
                m.x1[c, pl.ds(0, 2 * m.q)] = jnp.zeros((2 * m.q, H), BF)

            @pl.when(g == 7)
            def _():
                m.x1[c, pl.ds(10 * m.q, 2 * m.q)] = jnp.zeros((2 * m.q, H), BF)

            return carry

        lax.fori_loop(0, m.count, clear, 0)

    lower_first(small, 0)

    def at(p, stage):
        for c in range(int(stage is lower_first), FRONT + BACK):
            pl.when(p == (c if c < FRONT else c + BIG))(lambda c=c: stage(small, c))
        pl.when(jnp.logical_and(p >= FRONT, p < FRONT + BIG))(lambda: stage(big, p - FRONT))

    PLAN = [
        (near, 3), (pass_on, 5), (middle, 4), (far, 6),
        (lower_first, 0), (finish, 7), (send_halo, 1),
    ]

    def step(t, carry):
        for stage, lag in PLAN:
            at(t - lag, stage)
        return carry

    lax.fori_loop(0, CHUNKS + max(lag for _, lag in PLAN), step, 0)

    for m in (small, big):

        def drain(m, c):
            pl.when(g < 7)(lambda: halo_up(m, c).wait_send())
            pl.when(g > 0)(lambda: halo_down(m, c).wait_send())
            to_partner(m, c).wait_send()
            to_cross(m, c).wait_send()
            relay(m, c).wait_send()
            to_home(m, c).wait_send()
            for copy in stores(m, c):
                copy.wait()

        for c in range(m.count):
            drain(m, c)


def body(stream, bases, input_weight, kernel_weight, output_weight):
    hbm = pl.BlockSpec(memory_space=pl.ANY)
    vmem = pl.BlockSpec(memory_space=pltpu.VMEM)
    shape = (2, PITCH // 32, 32, D)
    result = pl.pallas_call(
        kernel,
        out_shape=jax.ShapeDtypeStruct(shape, BF),
        in_specs=[hbm, vmem, hbm, hbm, hbm],
        out_specs=hbm,
        scratch_shapes=[
            pltpu.VMEM((2, D, H), BF),
            pltpu.VMEM((2, TAPS * H, H), BF),
            pltpu.VMEM((2, H, D), BF),
            pltpu.SemaphoreType.DMA((6,)),
            *[ref for q, count in SETS for ref in Chunks(q, count, None).scratch()],
        ],
        compiler_params=pltpu.CompilerParams(
            collective_id=0, has_side_effects=True, vmem_limit_bytes=VMEM_LIMIT
        ),
    )(
        stream.reshape(shape),
        bases.reshape(14, 128),
        input_weight,
        kernel_weight.reshape(2, TAPS * H, H),
        output_weight,
    )
    return result.reshape(2 * PITCH, D)


def solution(mesh):
    return jax.shard_map(
        body,
        mesh=mesh,
        in_specs=(P(("batch", "seq"), None), P(("batch", "seq")), P(), P(), P()),
        out_specs=P(("batch", "seq"), None),
        check_vma=False,
    )
```

```python
import jax
import jax.numpy as jnp
from jax import lax
from jax.experimental import pallas as pl
from jax.experimental.pallas import tpu as pltpu
from jax.sharding import PartitionSpec as P

D, H, TAPS = 1280, 640, 5
PITCH = 896
FRONT, BIG, BACK = 1, 6, 1
CHUNKS = FRONT + BIG + BACK
BF, F32 = jnp.bfloat16, jnp.float32
VMEM_LIMIT = 54 * 2**20


def gelu_of_norm(v, mask=None):
    centre = v - jnp.mean(v, axis=-1, keepdims=True)
    scale = lax.rsqrt(jnp.mean(centre * centre, axis=-1, keepdims=True) + 1e-05)
    if mask is not None:
        scale = scale * mask
    u = centre * scale
    half = 0.5 * u
    bent = u * (0.7978845608028654 + 0.035677408136300125 * (u * u))
    return (half + half * jnp.tanh(bent)).astype(BF)


def dot(a, b):
    return jnp.dot(a, b, preferred_element_type=F32)


class Chunks:
    def __init__(self, q, count, refs):
        self.q, self.count = q, count
        self.rows, self.half = 8 * q, 4 * q
        if refs is None:
            return
        (
            self.sbuf, self.resid, self.pres, self.s1, self.x1, self.s2, self.a1, self.x2,
            self.load_sem, self.a_s, self.a_r, self.h_s, self.h_r,
            self.b_s, self.b_r, self.y_s, self.y_r,
        ) = refs

    def scratch(self):
        q, n = self.q, self.count
        dma = pltpu.SemaphoreType.DMA
        plain = pltpu.VMEM((n, self.rows, H), BF)
        return [
            pltpu.VMEM((n, 4, 2, q, D), BF),
            pltpu.VMEM((n, self.rows, D), F32),
            pltpu.VMEM((n, 4, 2, q, 1), F32),
            plain,
            pltpu.VMEM((n, 12 * q, H), BF),
            plain,
            plain,
            pltpu.VMEM((n, 6 * self.half, H), BF),
            dma((n, 8)),
            dma((n, 3)),
            dma((n, 3)),
            dma((n, 2)),
            dma((n, 2)),
            dma((n, 3)),
            dma((n, 3)),
            dma((n, 4)),
            dma((n, 4)),
        ]


SETS = ((16, FRONT + BACK), (32, max(BIG, 1)))
FIELDS = 17


def rows(start, size):
    return pl.ds(pl.multiple_of(start, 16), size)


def kernel(x_hbm, bases, win_hbm, kern_hbm, wout_hbm, out, win, kern, wout, w_sem, *refs):
    small = Chunks(*SETS[0], refs[:FIELDS])
    big = Chunks(*SETS[1], refs[FIELDS:])
    s = lax.axis_index("seq")
    y, g, z = s // 8, s // 4, s % 4
    low = y % 2
    upper = y // 2
    own_v = low + upper - 2 * low * upper
    partner = s + 8 - 16 * low
    cross = (3 - y) * 8 + s % 8
    base = s - z

    def remote(src, dst, send, recv, dev):
        return pltpu.make_async_remote_copy(
            src_ref=src, dst_ref=dst, send_sem=send, recv_sem=recv,
            device_id={"seq": dev}, device_id_type=pl.DeviceIdType.MESH,
        )

    def peer(k):
        return (z + k) % 4

    def gather(m, c, k):
        p, n = peer(k), 2 * m.q
        return remote(
            m.s1.at[c, rows(p * n, n)], m.x1.at[c, rows((1 + z) * n, n)],
            m.a_s.at[c, k - 1], m.a_r.at[c, k - 1], base + p,
        )

    def back(m, c, k):
        p, n = peer(k), 2 * m.q
        return remote(
            m.s2.at[c, rows(p * n, n)], m.a1.at[c, rows(z * n, n)],
            m.b_s.at[c, k - 1], m.b_r.at[c, k - 1], base + p,
        )

    def halo_up(m, c):
        n = 2 * m.q
        return remote(
            m.x1.at[c, pl.ds(4 * n, n)], m.x1.at[c, pl.ds(0, n)],
            m.h_s.at[c, 0], m.h_r.at[c, 0], s + 4,
        )

    def halo_down(m, c):
        n = 2 * m.q
        return remote(
            m.x1.at[c, pl.ds(n, n)], m.x1.at[c, pl.ds(5 * n, n)],
            m.h_s.at[c, 1], m.h_r.at[c, 1], s - 4,
        )

    def to_partner(m, c):
        return remote(
            m.s2.at[c, rows(own_v * m.half, m.half)], m.x2.at[c, rows((y + 1) * m.half, m.half)],
            m.y_s.at[c, 0], m.y_r.at[c, 0], partner,
        )

    def to_cross(m, c):
        return remote(
            m.s2.at[c, rows((1 - own_v) * m.half, m.half)], m.x2.at[c, rows((y + 1) * m.half, m.half)],
            m.y_s.at[c, 1], m.y_r.at[c, 1], cross,
        )

    def relay(m, c):
        part = m.x2.at[c, rows((y + 2 - 2 * low) * m.half, m.half)]
        return remote(part, part, m.y_s.at[c, 2], m.y_r.at[c, 2], cross)

    def to_home(m, c):
        return remote(
            m.s1.at[c, rows((1 - low) * m.half, m.half)], m.a1.at[c, rows((1 - own_v) * m.half, m.half)],
            m.y_s.at[c, 3], m.y_r.at[c, 3], partner,
        )

    def places(m, c):
        for h in range(2):
            if m is big:
                yield (h, pl.ds(2 * FRONT + 4 * c, 4)), (slice(None), h)
            else:
                behind = int(c >= FRONT) if isinstance(c, int) else (c >= FRONT).astype(jnp.int32)
                for i in range(4):
                    group = 2 * c + 4 * BIG * behind + i // 2
                    yield (h, group, pl.ds(16 * (i % 2), 16)), (i, h)

    def loads(m, c):
        return [
            pltpu.make_async_copy(x_hbm.at[there], m.sbuf.at[(c, *here)], m.load_sem.at[c, i])
            for i, (there, here) in enumerate(places(m, c))
        ]

    weights = {
        "in0": pltpu.make_async_copy(win_hbm.at[0], win.at[0], w_sem.at[0]),
        "k0": pltpu.make_async_copy(kern_hbm.at[0], kern.at[0], w_sem.at[1]),
        "out0": pltpu.make_async_copy(wout_hbm.at[0], wout.at[0], w_sem.at[2]),
        "in1": pltpu.make_async_copy(win_hbm.at[1], win.at[1], w_sem.at[3]),
        "k1": pltpu.make_async_copy(kern_hbm.at[1], kern.at[1], w_sem.at[4]),
        "out1": pltpu.make_async_copy(wout_hbm.at[1], wout.at[1], w_sem.at[5]),
    }

    def first(m, c, *names):
        if m is small:

            @pl.when(c == 0)
            def _():
                for name in names:
                    weights[name].wait()

    def lower_first(m, c):
        for copy in loads(m, c):
            copy.wait()
        if isinstance(c, int):
            first(m, c, "in0")
        v = m.sbuf[c].reshape(m.rows, D).astype(F32)
        lowered = dot(gelu_of_norm(v), win[0])
        m.s1[c] = gelu_of_norm(lowered, m.pres[c].reshape(m.rows, 1))

    def send_first(m, c):
        for k in (2, 1, 3):
            gather(m, c, k).start()
        n = 2 * m.q
        m.x1[c, rows((1 + z) * n, n)] = m.s1[c, rows(z * n, n)]

    def send_halo(m, c):
        for k in (1, 2, 3):
            gather(m, c, k).wait_recv()
        pl.when(g < 7)(lambda: halo_up(m, c).start())
        pl.when(g > 0)(lambda: halo_down(m, c).start())

    def near(m, c):
        first(m, c, "k0")
        pl.when(g > 0)(lambda: halo_up(m, c).wait_recv())
        pl.when(g < 7)(lambda: halo_down(m, c).wait_recv())
        wide = jnp.concatenate([m.x1[c, pl.ds(k * m.q, 8 * m.q)] for k in range(TAPS)], axis=1)
        m.s2[c] = gelu_of_norm(dot(wide, kern[0]))
        for k in (2, 1, 3):
            back(m, c, k).start()
        n = 2 * m.q
        m.a1[c, rows(z * n, n)] = m.s2[c, rows(z * n, n)]

    def middle(m, c):
        first(m, c, "out0", "in1")
        for k in (1, 2, 3):
            back(m, c, k).wait_recv()
        m.resid[c] = m.sbuf[c].reshape(m.rows, D).astype(F32) + dot(m.a1[c], wout[0])
        lowered = dot(gelu_of_norm(m.resid[c]), win[1])
        for k in (1, 2, 3):
            back(m, c, k).wait_send()
        m.s2[c] = gelu_of_norm(lowered, m.pres[c].reshape(m.rows, 1))
        to_partner(m, c).start()
        to_cross(m, c).start()
        m.x2[c, rows((y + 1) * m.half, m.half)] = m.s2[c, rows((1 - own_v) * m.half, m.half)]

    def pass_on(m, c):
        to_partner(m, c).wait_recv()
        relay(m, c).start()

    def far(m, c):
        first(m, c, "k1")
        to_cross(m, c).wait_recv()
        relay(m, c).wait_recv()
        for k in (1, 2, 3):
            gather(m, c, k).wait_send()
        wide = jnp.concatenate(
            [m.x2[c, rows((upper + k) * m.half, m.rows)] for k in range(4)], axis=1
        )
        m.s1[c] = gelu_of_norm(dot(wide, kern[1, rows((1 - upper) * H, 4 * H)]))
        to_home(m, c).start()
        m.a1[c, rows((1 - own_v) * m.half, m.half)] = m.s1[c, rows(low * m.half, m.half)]

    def finish(m, c):
        first(m, c, "out1")
        to_home(m, c).wait_recv()
        result = m.resid[c] + dot(m.a1[c], wout[1])
        result = result.astype(BF).reshape(4, 2, m.q, D)
        for there, here in places(m, c):
            out[there] = result[here]

    barrier = pltpu.get_barrier_semaphore()

    def greet(dev):
        pl.semaphore_signal(barrier, inc=1, device_id={"seq": dev}, device_id_type=pl.DeviceIdType.MESH)

    for k in (1, 2, 3):
        greet(base + peer(k))
    greet(partner)
    greet(cross)
    pl.when(g < 7)(lambda: greet(s + 4))
    pl.when(g > 0)(lambda: greet(s - 4))

    order = [(small, c) for c in range(FRONT)]
    order += [(big, c) for c in range(BIG)]
    order += [(small, c) for c in range(FRONT, FRONT + BACK)]
    for i, (m, c) in enumerate(order):
        for copy in loads(m, c):
            copy.start()
        if i == 0:
            weights["in0"].start()
        if i == 1:
            weights["k0"].start()
        if i == 2:
            weights["out0"].start()
            weights["in1"].start()
    weights["k1"].start()
    weights["out1"].start()

    known = (bases[...] != 4).astype(F32).T
    for c, (m, i) in enumerate(order):
        n = 4 * m.q
        start = 64 * c if c <= FRONT else 64 * FRONT + 128 * (c - FRONT)
        if c > FRONT + BIG:
            start = 64 * (c - BIG) + 128 * BIG
        for h in range(2):
            for j in range(4):
                at = start + j * m.q
                col = h * 7 + at // 128
                m.pres[i, j, h] = known[at % 128 : at % 128 + m.q, col : col + 1]

    for m in (small, big):

        def clear(c, carry):
            m.x2[c, pl.ds(0, m.half)] = jnp.zeros((m.half, H), BF)
            m.x2[c, pl.ds(5 * m.half, m.half)] = jnp.zeros((m.half, H), BF)

            @pl.when(g == 0)
            def _():
                m.x1[c, pl.ds(0, 2 * m.q)] = jnp.zeros((2 * m.q, H), BF)

            @pl.when(g == 7)
            def _():
                m.x1[c, pl.ds(10 * m.q, 2 * m.q)] = jnp.zeros((2 * m.q, H), BF)

            return carry

        lax.fori_loop(0, m.count if m is small else BIG, clear, 0)

    early = order[:2]
    for m, c in early:
        lower_first(m, c)
    pl.semaphore_wait(barrier, 5 + (g + 6) // 7 + (13 - g) // 7)
    for m, c in early:
        send_first(m, c)

    def at(p, stage):
        if stage is lower_first:
            p = p + jnp.where(p < 2, CHUNKS, 0)

        def short():
            run(small, p - BIG * (p >= FRONT).astype(jnp.int32))

        def run(m, c):
            stage(m, c)
            if stage is lower_first:
                send_first(m, c)

        if BIG:
            in_front = jnp.logical_and(p >= 0, p < FRONT)
            in_back = jnp.logical_and(p >= FRONT + BIG, p < CHUNKS)
            pl.when(jnp.logical_or(in_front, in_back))(short)
            pl.when(jnp.logical_and(p >= FRONT, p < FRONT + BIG))(lambda: run(big, p - FRONT))
        else:
            pl.when(jnp.logical_and(p >= 0, p < CHUNKS))(short)

    PLAN = [
        (near, 3),
        (pass_on, 5),
        (middle, 4),
        (far, 6),
        (lower_first, 0),
        (finish, 7),
        (send_halo, 1),
    ]

    def step(t, carry):
        for stage, lag in PLAN:
            at(t - lag, stage)
        return carry

    lax.fori_loop(0, CHUNKS + max(lag for _, lag in PLAN), step, 0)

    for m in (small, big):

        def drain(m, c):
            pl.when(g < 7)(lambda: halo_up(m, c).wait_send())
            pl.when(g > 0)(lambda: halo_down(m, c).wait_send())
            to_partner(m, c).wait_send()
            to_cross(m, c).wait_send()
            relay(m, c).wait_send()
            to_home(m, c).wait_send()

        lax.fori_loop(0, m.count if m is small else BIG, lambda c, carry: (drain(m, c), carry)[1], 0)


def body(stream, bases, input_weight, kernel_weight, output_weight):
    hbm = pl.BlockSpec(memory_space=pl.ANY)
    vmem = pl.BlockSpec(memory_space=pltpu.VMEM)
    shape = (2, PITCH // 32, 32, D)
    result = pl.pallas_call(
        kernel,
        out_shape=pltpu.VMEM(shape, BF),
        in_specs=[hbm, vmem, hbm, hbm, hbm],
        out_specs=vmem,
        scratch_shapes=[
            pltpu.VMEM((2, D, H), BF),
            pltpu.VMEM((2, TAPS * H, H), BF),
            pltpu.VMEM((2, H, D), BF),
            pltpu.SemaphoreType.DMA((6,)),
            *[ref for q, count in SETS for ref in Chunks(q, count, None).scratch()],
        ],
        compiler_params=pltpu.CompilerParams(
            collective_id=0, has_side_effects=True, vmem_limit_bytes=VMEM_LIMIT
        ),
    )(
        stream.reshape(shape),
        bases.reshape(14, 128),
        input_weight,
        kernel_weight.reshape(2, TAPS * H, H),
        output_weight,
    )
    return result.reshape(2 * PITCH, D)


def solution(mesh):
    return jax.shard_map(
        body,
        mesh=mesh,
        in_specs=(P(("batch", "seq"), None), P(("batch", "seq")), P(), P(), P()),
        out_specs=P(("batch", "seq"), None),
        check_vma=False,
    )
```

```python
import jax
import jax.numpy as jnp
from jax import lax
from jax.experimental import pallas as pl
from jax.experimental.pallas import tpu as pltpu
from jax.sharding import PartitionSpec as P

D, H, TAPS = 1280, 640, 5
PITCH = 896
FRONT, BIG, BACK = 1, 6, 1
CHUNKS = FRONT + BIG + BACK
BF, F32 = jnp.bfloat16, jnp.float32
PARTS = 2
VMEM_LIMIT = 54 * 2**20


def gelu_of_norm(v, mask=None):
    centre = v - jnp.mean(v, axis=-1, keepdims=True)
    scale = lax.rsqrt(jnp.mean(centre * centre, axis=-1, keepdims=True) + 1e-05)
    if mask is not None:
        scale = scale * mask
    u = centre * scale
    half = 0.5 * u
    bent = u * (0.7978845608028654 + 0.035677408136300125 * (u * u))
    return (half + half * jnp.tanh(bent)).astype(BF)


def dot(a, b):
    return jnp.dot(a, b, preferred_element_type=F32)


class Chunks:
    def __init__(self, q, count, refs):
        self.q, self.count = q, count
        self.rows, self.half = 8 * q, 4 * q
        count = PARTS if q == 32 else 1
        size = self.rows // count
        self.parts = [slice(i * size, (i + 1) * size) for i in range(count)]
        if refs is None:
            return
        (
            self.sbuf, self.resid, self.pres, self.s1, self.x1, self.s2, self.a1, self.x2,
            self.load_sem, self.a_s, self.a_r, self.h_s, self.h_r,
            self.b_s, self.b_r, self.y_s, self.y_r,
        ) = refs

    def scratch(self):
        q, n = self.q, self.count
        dma = pltpu.SemaphoreType.DMA
        plain = pltpu.VMEM((n, self.rows, H), BF)
        return [
            pltpu.VMEM((n, 4, 2, q, D), BF),
            pltpu.VMEM((n, self.rows, D), F32),
            pltpu.VMEM((n, 4, 2, q, 1), F32),
            plain,
            pltpu.VMEM((n, 12 * q, H), BF),
            plain,
            plain,
            pltpu.VMEM((n, 6 * self.half, H), BF),
            dma((n, 8)),
            dma((n, 3)),
            dma((n, 3)),
            dma((n, 2)),
            dma((n, 2)),
            dma((n, 3)),
            dma((n, 3)),
            dma((n, 4)),
            dma((n, 4)),
        ]


SETS = ((16, FRONT + BACK), (32, max(BIG, 1)))
FIELDS = 17


def rows(start, size):
    return pl.ds(pl.multiple_of(start, 16), size)


def kernel(x_hbm, bases, win_hbm, kern_hbm, wout_hbm, out, win, kern, wout, w_sem, *refs):
    small = Chunks(*SETS[0], refs[:FIELDS])
    big = Chunks(*SETS[1], refs[FIELDS:])
    s = lax.axis_index("seq")
    y, g, z = s // 8, s // 4, s % 4
    low = y % 2
    upper = y // 2
    own_v = low + upper - 2 * low * upper
    partner = s + 8 - 16 * low
    cross = (3 - y) * 8 + s % 8
    batch = lax.axis_index("batch")
    peers = [(z + k) % 4 for k in range(4)]
    ring = [s - z + p for p in peers]
    own_slot, partner_slot = y + 1, y + 2 - 2 * low
    keep, give = 1 - own_v, own_v

    def remote(src, dst, send, recv, dev):
        return pltpu.make_async_remote_copy(
            src_ref=src, dst_ref=dst, send_sem=send, recv_sem=recv,
            device_id=(dev, batch), device_id_type=pl.DeviceIdType.MESH,
        )

    def gather(m, c, k):
        p, n = peers[k], 2 * m.q
        return remote(
            m.s1.at[c, rows(p * n, n)], m.x1.at[c, rows((1 + z) * n, n)],
            m.a_s.at[c, k - 1], m.a_r.at[c, k - 1], ring[k],
        )

    def back(m, c, k):
        p, n = peers[k], 2 * m.q
        return remote(
            m.s2.at[c, rows(p * n, n)], m.a1.at[c, rows(z * n, n)],
            m.b_s.at[c, k - 1], m.b_r.at[c, k - 1], ring[k],
        )

    def halo_up(m, c):
        n = 2 * m.q
        return remote(
            m.x1.at[c, pl.ds(4 * n, n)], m.x1.at[c, pl.ds(0, n)],
            m.h_s.at[c, 0], m.h_r.at[c, 0], s + 4,
        )

    def halo_down(m, c):
        n = 2 * m.q
        return remote(
            m.x1.at[c, pl.ds(n, n)], m.x1.at[c, pl.ds(5 * n, n)],
            m.h_s.at[c, 1], m.h_r.at[c, 1], s - 4,
        )

    def to_partner(m, c):
        return remote(
            m.s2.at[c, rows(give * m.half, m.half)], m.x2.at[c, rows(own_slot * m.half, m.half)],
            m.y_s.at[c, 0], m.y_r.at[c, 0], partner,
        )

    def to_cross(m, c):
        return remote(
            m.s2.at[c, rows(keep * m.half, m.half)], m.x2.at[c, rows(own_slot * m.half, m.half)],
            m.y_s.at[c, 1], m.y_r.at[c, 1], cross,
        )

    def relay(m, c):
        part = m.x2.at[c, rows(partner_slot * m.half, m.half)]
        return remote(part, part, m.y_s.at[c, 2], m.y_r.at[c, 2], cross)

    def to_home(m, c):
        return remote(
            m.s1.at[c, rows((1 - low) * m.half, m.half)], m.a1.at[c, rows(keep * m.half, m.half)],
            m.y_s.at[c, 3], m.y_r.at[c, 3], partner,
        )

    def places(m, c):
        for h in range(2):
            if m is big:
                yield (h, pl.ds(2 * FRONT + 4 * c, 4)), (slice(None), h)
            else:
                behind = int(c >= FRONT) if isinstance(c, int) else (c >= FRONT).astype(jnp.int32)
                for i in range(4):
                    group = 2 * c + 4 * BIG * behind + i // 2
                    yield (h, group, pl.ds(16 * (i % 2), 16)), (i, h)

    def loads(m, c):
        return [
            pltpu.make_async_copy(x_hbm.at[there], m.sbuf.at[(c, *here)], m.load_sem.at[c, i])
            for i, (there, here) in enumerate(places(m, c))
        ]

    weights = {
        "in0": pltpu.make_async_copy(win_hbm.at[0], win.at[0], w_sem.at[0]),
        "k0": pltpu.make_async_copy(kern_hbm.at[0], kern.at[0], w_sem.at[1]),
        "out0": pltpu.make_async_copy(wout_hbm.at[0], wout.at[0], w_sem.at[2]),
        "in1": pltpu.make_async_copy(win_hbm.at[1], win.at[1], w_sem.at[3]),
        "k1": pltpu.make_async_copy(kern_hbm.at[1], kern.at[1], w_sem.at[4]),
        "out1": pltpu.make_async_copy(wout_hbm.at[1], wout.at[1], w_sem.at[5]),
    }

    def first(m, c, *names):
        if m is small:

            @pl.when(c == 0)
            def _():
                for name in names:
                    weights[name].wait()

    def lower_first(m, c):
        for copy in loads(m, c):
            copy.wait()
        if isinstance(c, int):
            first(m, c, "in0")
        mask = m.pres[c].reshape(m.rows, 1)
        v = m.sbuf[c].reshape(m.rows, D)
        normed = [gelu_of_norm(v[part].astype(F32)) for part in m.parts]
        lowered = [dot(n, win[0]) for n in normed]
        for part, low_part in zip(m.parts, lowered):
            m.s1[c, part] = gelu_of_norm(low_part, mask[part])

    def send_first(m, c):
        for k in (2, 1, 3):
            gather(m, c, k).start()
        n = 2 * m.q
        m.x1[c, rows((1 + z) * n, n)] = m.s1[c, rows(z * n, n)]

    def send_halo(m, c):
        for k in (1, 2, 3):
            gather(m, c, k).wait_recv()
        pl.when(g < 7)(lambda: halo_up(m, c).start())
        pl.when(g > 0)(lambda: halo_down(m, c).start())

    def near(m, c):
        first(m, c, "k0")
        pl.when(g > 0)(lambda: halo_up(m, c).wait_recv())
        pl.when(g < 7)(lambda: halo_down(m, c).wait_recv())
        for part in m.parts:
            size = part.stop - part.start
            wide = [m.x1[c, pl.ds(k * m.q + part.start, size)] for k in range(TAPS)]
            m.s2[c, part] = gelu_of_norm(dot(jnp.concatenate(wide, axis=1), kern[0]))
        for k in (2, 1, 3):
            back(m, c, k).start()
        n = 2 * m.q
        m.a1[c, rows(z * n, n)] = m.s2[c, rows(z * n, n)]

    def middle(m, c):
        first(m, c, "out0", "in1")
        for k in (1, 2, 3):
            back(m, c, k).wait_recv()
        for k in (1, 2, 3):
            back(m, c, k).wait_send()
        mask = m.pres[c].reshape(m.rows, 1)
        v = m.sbuf[c].reshape(m.rows, D)
        normed = []
        for part in m.parts:
            total = v[part].astype(F32) + dot(m.a1[c, part], wout[0])
            m.resid[c, part] = total
            normed.append(gelu_of_norm(total))
        lowered = [dot(n, win[1]) for n in normed]
        for part, low_part in zip(m.parts, lowered):
            m.s2[c, part] = gelu_of_norm(low_part, mask[part])
        to_partner(m, c).start()
        to_cross(m, c).start()
        m.x2[c, rows(own_slot * m.half, m.half)] = m.s2[c, rows(keep * m.half, m.half)]

    def pass_on(m, c):
        to_partner(m, c).wait_recv()
        relay(m, c).start()

    def far(m, c):
        first(m, c, "k1")
        to_cross(m, c).wait_recv()
        relay(m, c).wait_recv()
        for k in (1, 2, 3):
            gather(m, c, k).wait_send()
        for part in m.parts:
            size = part.stop - part.start
            wide = [m.x2[c, rows((upper + k) * m.half + part.start, size)] for k in range(4)]
            wide = jnp.concatenate(wide, axis=1)
            m.s1[c, part] = gelu_of_norm(dot(wide, kern[1, rows((1 - upper) * H, 4 * H)]))
        to_home(m, c).start()
        m.a1[c, rows(keep * m.half, m.half)] = m.s1[c, rows(low * m.half, m.half)]

    def finish(m, c):
        first(m, c, "out1")
        to_home(m, c).wait_recv()
        result = m.resid[c] + dot(m.a1[c], wout[1])
        result = result.astype(BF).reshape(4, 2, m.q, D)
        for there, here in places(m, c):
            out[there] = result[here]

    barrier = pltpu.get_barrier_semaphore()

    def greet(dev):
        pl.semaphore_signal(barrier, inc=1, device_id=(dev, batch), device_id_type=pl.DeviceIdType.MESH)

    for k in (1, 2, 3):
        greet(ring[k])
    greet(partner)
    greet(cross)
    pl.when(g < 7)(lambda: greet(s + 4))
    pl.when(g > 0)(lambda: greet(s - 4))

    order = [(small, c) for c in range(FRONT)]
    order += [(big, c) for c in range(BIG)]
    order += [(small, c) for c in range(FRONT, FRONT + BACK)]
    def fetch(some):
        for m, c in some:
            for copy in loads(m, c):
                copy.start()

    fetch(order[:1])
    weights["in0"].start()
    fetch(order[1:2])

    known = (bases[...] != 4).astype(F32).T
    for c, (m, i) in enumerate(order):
        n = 4 * m.q
        start = 64 * c if c <= FRONT else 64 * FRONT + 128 * (c - FRONT)
        if c > FRONT + BIG:
            start = 64 * (c - BIG) + 128 * BIG
        for h in range(2):
            for j in range(4):
                at = start + j * m.q
                col = h * 7 + at // 128
                m.pres[i, j, h] = known[at % 128 : at % 128 + m.q, col : col + 1]

    for m in (small, big):

        def clear(c, carry):
            m.x2[c, pl.ds(0, m.half)] = jnp.zeros((m.half, H), BF)
            m.x2[c, pl.ds(5 * m.half, m.half)] = jnp.zeros((m.half, H), BF)

            @pl.when(g == 0)
            def _():
                m.x1[c, pl.ds(0, 2 * m.q)] = jnp.zeros((2 * m.q, H), BF)

            @pl.when(g == 7)
            def _():
                m.x1[c, pl.ds(10 * m.q, 2 * m.q)] = jnp.zeros((2 * m.q, H), BF)

            return carry

        lax.fori_loop(0, m.count if m is small else BIG, clear, 0)

    early = order[:2]
    lower_first(*early[0])
    weights["k0"].start()
    fetch(order[2:4])
    for name in ("out0", "in1"):
        weights[name].start()
    fetch(order[4:])
    for name in ("k1", "out1"):
        weights[name].start()
    lower_first(*early[1])
    pl.semaphore_wait(barrier, 5 + (g + 6) // 7 + (13 - g) // 7)
    for m, c in early:
        send_first(m, c)

    def at(p, stage):
        if stage is lower_first:
            p = p + jnp.where(p < 2, CHUNKS, 0)

        def short():
            run(small, p - BIG * (p >= FRONT).astype(jnp.int32))

        def run(m, c):
            stage(m, c)
            if stage is lower_first:
                send_first(m, c)

        if BIG:
            in_front = jnp.logical_and(p >= 0, p < FRONT)
            in_back = jnp.logical_and(p >= FRONT + BIG, p < CHUNKS)
            pl.when(jnp.logical_or(in_front, in_back))(short)
            pl.when(jnp.logical_and(p >= FRONT, p < FRONT + BIG))(lambda: run(big, p - FRONT))
        else:
            pl.when(jnp.logical_and(p >= 0, p < CHUNKS))(short)

    PLAN = [
        (near, 3),
        (pass_on, 5),
        (middle, 4),
        (far, 6),
        (lower_first, 0),
        (finish, 7),
        (send_halo, 1),
    ]

    def step(t, carry):
        for stage, lag in PLAN:
            at(t - lag, stage)
        return carry

    lax.fori_loop(0, CHUNKS + max(lag for _, lag in PLAN), step, 0)

    for m in (small, big):

        def drain(m, c):
            pl.when(g < 7)(lambda: halo_up(m, c).wait_send())
            pl.when(g > 0)(lambda: halo_down(m, c).wait_send())
            to_partner(m, c).wait_send()
            to_cross(m, c).wait_send()
            relay(m, c).wait_send()
            to_home(m, c).wait_send()

        lax.fori_loop(0, m.count if m is small else BIG, lambda c, carry: (drain(m, c), carry)[1], 0)


def body(stream, bases, input_weight, kernel_weight, output_weight):
    hbm = pl.BlockSpec(memory_space=pl.ANY)
    vmem = pl.BlockSpec(memory_space=pltpu.VMEM)
    shape = (2, PITCH // 32, 32, D)
    result = pl.pallas_call(
        kernel,
        out_shape=pltpu.VMEM(shape, BF),
        in_specs=[hbm, vmem, hbm, hbm, hbm],
        out_specs=vmem,
        scratch_shapes=[
            pltpu.VMEM((2, D, H), BF),
            pltpu.VMEM((2, TAPS * H, H), BF),
            pltpu.VMEM((2, H, D), BF),
            pltpu.SemaphoreType.DMA((6,)),
            *[ref for q, count in SETS for ref in Chunks(q, count, None).scratch()],
        ],
        compiler_params=pltpu.CompilerParams(
            collective_id=0, has_side_effects=True, vmem_limit_bytes=VMEM_LIMIT
        ),
    )(
        stream.reshape(shape),
        bases.reshape(14, 128),
        input_weight,
        kernel_weight.reshape(2, TAPS * H, H),
        output_weight,
    )
    return result.reshape(2 * PITCH, D)


def solution(mesh):
    return jax.shard_map(
        body,
        mesh=mesh,
        in_specs=(P(("batch", "seq"), None), P(("batch", "seq")), P(), P(), P()),
        out_specs=P(("batch", "seq"), None),
        check_vma=False,
    )
```

```python
import jax
import jax.numpy as jnp
from jax import lax
from jax.experimental import pallas as pl
from jax.experimental.pallas import tpu as pltpu
from jax.sharding import PartitionSpec as P

D, H, TAPS = 1280, 640, 5
PITCH = 896
FRONT, BIG, BACK = 1, 6, 1
CHUNKS = FRONT + BIG + BACK
BF, F32 = jnp.bfloat16, jnp.float32
PARTS = 2
VMEM_LIMIT = 54 * 2**20


def gelu_of_norm(v, mask=None):
    centre = v - jnp.mean(v, axis=-1, keepdims=True)
    scale = lax.rsqrt(jnp.mean(centre * centre, axis=-1, keepdims=True) + 1e-05)
    if mask is not None:
        scale = scale * mask
    u = centre * scale
    half = 0.5 * u
    bent = u * (0.7978845608028654 + 0.035677408136300125 * (u * u))
    return (half + half * jnp.tanh(bent)).astype(BF)


def dot(a, b):
    return jnp.dot(a, b, preferred_element_type=F32)


class Chunks:
    def __init__(self, q, count, refs):
        self.q, self.count = q, count
        self.rows, self.half = 8 * q, 4 * q
        count = PARTS if q == 32 else 1
        size = self.rows // count
        self.parts = [slice(i * size, (i + 1) * size) for i in range(count)]
        if refs is None:
            return
        (
            self.sbuf, self.resid, self.pres, self.s1, self.x1, self.s2, self.a1, self.x2,
            self.load_sem, self.a_s, self.a_r, self.h_s, self.h_r,
            self.b_s, self.b_r, self.y_s, self.y_r,
        ) = refs

    def scratch(self):
        q, n = self.q, self.count
        dma = pltpu.SemaphoreType.DMA
        plain = pltpu.VMEM((n, self.rows, H), BF)
        return [
            pltpu.VMEM((n, 4, 2, q, D), BF),
            pltpu.VMEM((n, self.rows, D), F32),
            pltpu.VMEM((n, 4, 2, q, 1), F32),
            plain,
            pltpu.VMEM((n, 12 * q, H), BF),
            plain,
            plain,
            pltpu.VMEM((n, 6 * self.half, H), BF),
            dma((n, 8)),
            dma((n, 3)),
            dma((n, 3)),
            dma((n, 2)),
            dma((n, 2)),
            dma((n, 3)),
            dma((n, 3)),
            dma((n, 4)),
            dma((n, 4)),
        ]


SETS = ((16, FRONT + BACK), (32, max(BIG, 1)))
FIELDS = 17


def rows(start, size):
    return pl.ds(pl.multiple_of(start, 16), size)


def kernel(x_hbm, bases, win_hbm, kern_hbm, wout_hbm, out, win, kern, wout, w_sem, *refs):
    small = Chunks(*SETS[0], refs[:FIELDS])
    big = Chunks(*SETS[1], refs[FIELDS:])
    s = lax.axis_index("seq")
    y, g, z = s // 8, s // 4, s % 4
    low = y % 2
    upper = y // 2
    own_v = low + upper - 2 * low * upper
    partner = s + 8 - 16 * low
    cross = (3 - y) * 8 + s % 8
    batch = lax.axis_index("batch")
    peers = [(z + k) % 4 for k in range(4)]
    ring = [s - z + p for p in peers]
    own_slot, partner_slot = y + 1, y + 2 - 2 * low
    keep, give = 1 - own_v, own_v

    def remote(src, dst, send, recv, dev):
        return pltpu.make_async_remote_copy(
            src_ref=src, dst_ref=dst, send_sem=send, recv_sem=recv,
            device_id=(dev, batch), device_id_type=pl.DeviceIdType.MESH,
        )

    def gather(m, c, k):
        p, n = peers[k], 2 * m.q
        return remote(
            m.s1.at[c, rows(p * n, n)], m.x1.at[c, rows((1 + z) * n, n)],
            m.a_s.at[c, k - 1], m.a_r.at[c, k - 1], ring[k],
        )

    def back(m, c, k):
        p, n = peers[k], 2 * m.q
        return remote(
            m.s2.at[c, rows(p * n, n)], m.a1.at[c, rows(z * n, n)],
            m.b_s.at[c, k - 1], m.b_r.at[c, k - 1], ring[k],
        )

    def halo_up(m, c):
        n = 2 * m.q
        return remote(
            m.x1.at[c, pl.ds(4 * n, n)], m.x1.at[c, pl.ds(0, n)],
            m.h_s.at[c, 0], m.h_r.at[c, 0], s + 4,
        )

    def halo_down(m, c):
        n = 2 * m.q
        return remote(
            m.x1.at[c, pl.ds(n, n)], m.x1.at[c, pl.ds(5 * n, n)],
            m.h_s.at[c, 1], m.h_r.at[c, 1], s - 4,
        )

    def to_partner(m, c):
        return remote(
            m.s2.at[c, rows(give * m.half, m.half)], m.x2.at[c, rows(own_slot * m.half, m.half)],
            m.y_s.at[c, 0], m.y_r.at[c, 0], partner,
        )

    def to_cross(m, c):
        return remote(
            m.s2.at[c, rows(keep * m.half, m.half)], m.x2.at[c, rows(own_slot * m.half, m.half)],
            m.y_s.at[c, 1], m.y_r.at[c, 1], cross,
        )

    def relay(m, c):
        part = m.x2.at[c, rows(partner_slot * m.half, m.half)]
        return remote(part, part, m.y_s.at[c, 2], m.y_r.at[c, 2], cross)

    def to_home(m, c):
        return remote(
            m.s1.at[c, rows((1 - low) * m.half, m.half)], m.a1.at[c, rows(keep * m.half, m.half)],
            m.y_s.at[c, 3], m.y_r.at[c, 3], partner,
        )

    def places(m, c):
        for h in range(2):
            if m is big:
                yield (h, pl.ds(2 * FRONT + 4 * c, 4)), (slice(None), h)
            else:
                behind = int(c >= FRONT) if isinstance(c, int) else (c >= FRONT).astype(jnp.int32)
                for i in range(4):
                    group = 2 * c + 4 * BIG * behind + i // 2
                    yield (h, group, pl.ds(16 * (i % 2), 16)), (i, h)

    def loads(m, c):
        return [
            pltpu.make_async_copy(x_hbm.at[there], m.sbuf.at[(c, *here)], m.load_sem.at[c, i])
            for i, (there, here) in enumerate(places(m, c))
        ]

    weights = {
        "in0": pltpu.make_async_copy(win_hbm.at[0], win.at[0], w_sem.at[0]),
        "k0": pltpu.make_async_copy(kern_hbm.at[0], kern.at[0], w_sem.at[1]),
        "out0": pltpu.make_async_copy(wout_hbm.at[0], wout.at[0], w_sem.at[2]),
        "in1": pltpu.make_async_copy(win_hbm.at[1], win.at[1], w_sem.at[3]),
        "k1": pltpu.make_async_copy(kern_hbm.at[1], kern.at[1], w_sem.at[4]),
        "out1": pltpu.make_async_copy(wout_hbm.at[1], wout.at[1], w_sem.at[5]),
    }

    def first(m, c, *names):
        if m is small:

            @pl.when(c == 0)
            def _():
                for name in names:
                    weights[name].wait()

    def lower_first(m, c):
        for copy in loads(m, c):
            copy.wait()
        if isinstance(c, int):
            first(m, c, "in0")
        mask = m.pres[c].reshape(m.rows, 1)
        v = m.sbuf[c].reshape(m.rows, D)
        normed = [gelu_of_norm(v[part].astype(F32)) for part in m.parts]
        lowered = [dot(n, win[0]) for n in normed]
        for part, low_part in zip(m.parts, lowered):
            m.s1[c, part] = gelu_of_norm(low_part, mask[part])

    def send_first(m, c):
        for k in (2, 1, 3):
            gather(m, c, k).start()
        n = 2 * m.q
        m.x1[c, rows((1 + z) * n, n)] = m.s1[c, rows(z * n, n)]

    def send_halo(m, c):
        for k in (1, 2, 3):
            gather(m, c, k).wait_recv()
        pl.when(g < 7)(lambda: halo_up(m, c).start())
        pl.when(g > 0)(lambda: halo_down(m, c).start())

    def near(m, c):
        first(m, c, "k0")
        pl.when(g > 0)(lambda: halo_up(m, c).wait_recv())
        pl.when(g < 7)(lambda: halo_down(m, c).wait_recv())
        for part in m.parts:
            size = part.stop - part.start
            wide = [m.x1[c, pl.ds(k * m.q + part.start, size)] for k in range(TAPS)]
            m.s2[c, part] = gelu_of_norm(dot(jnp.concatenate(wide, axis=1), kern[0]))
        for k in (2, 1, 3):
            back(m, c, k).start()
        n = 2 * m.q
        m.a1[c, rows(z * n, n)] = m.s2[c, rows(z * n, n)]

    def middle(m, c):
        first(m, c, "out0", "in1")
        for k in (1, 2, 3):
            back(m, c, k).wait_recv()
        for k in (1, 2, 3):
            back(m, c, k).wait_send()
        for which, send in ((give, to_partner), (keep, to_cross)):
            part, runs = rows(which * m.half, m.half), pl.ds(2 * which, 2)
            v = m.sbuf[c, runs].reshape(m.half, D)
            total = v.astype(F32) + dot(m.a1[c, part], wout[0])
            m.resid[c, part] = total
            lowered = dot(gelu_of_norm(total), win[1])
            m.s2[c, part] = gelu_of_norm(lowered, m.pres[c, runs].reshape(m.half, 1))
            send(m, c).start()
        m.x2[c, rows(own_slot * m.half, m.half)] = m.s2[c, rows(keep * m.half, m.half)]

    def pass_on(m, c):
        to_partner(m, c).wait_recv()
        relay(m, c).start()

    def far(m, c):
        first(m, c, "k1")
        to_cross(m, c).wait_recv()
        relay(m, c).wait_recv()
        for k in (1, 2, 3):
            gather(m, c, k).wait_send()
        for part in m.parts:
            size = part.stop - part.start
            wide = [m.x2[c, rows((upper + k) * m.half + part.start, size)] for k in range(4)]
            wide = jnp.concatenate(wide, axis=1)
            m.s1[c, part] = gelu_of_norm(dot(wide, kern[1, rows((1 - upper) * H, 4 * H)]))
        to_home(m, c).start()
        m.a1[c, rows(keep * m.half, m.half)] = m.s1[c, rows(low * m.half, m.half)]

    def finish(m, c):
        first(m, c, "out1")
        to_home(m, c).wait_recv()
        result = m.resid[c] + dot(m.a1[c], wout[1])
        result = result.astype(BF).reshape(4, 2, m.q, D)
        for there, here in places(m, c):
            out[there] = result[here]

    barrier = pltpu.get_barrier_semaphore()

    def greet(dev):
        pl.semaphore_signal(barrier, inc=1, device_id=(dev, batch), device_id_type=pl.DeviceIdType.MESH)

    for k in (1, 2, 3):
        greet(ring[k])
    greet(partner)
    greet(cross)
    pl.when(g < 7)(lambda: greet(s + 4))
    pl.when(g > 0)(lambda: greet(s - 4))

    order = [(small, c) for c in range(FRONT)]
    order += [(big, c) for c in range(BIG)]
    order += [(small, c) for c in range(FRONT, FRONT + BACK)]
    def fetch(some):
        for m, c in some:
            for copy in loads(m, c):
                copy.start()

    fetch(order[:1])
    weights["in0"].start()
    fetch(order[1:2])

    known = (bases[...] != 4).astype(F32).T
    for c, (m, i) in enumerate(order):
        n = 4 * m.q
        start = 64 * c if c <= FRONT else 64 * FRONT + 128 * (c - FRONT)
        if c > FRONT + BIG:
            start = 64 * (c - BIG) + 128 * BIG
        for h in range(2):
            for j in range(4):
                at = start + j * m.q
                col = h * 7 + at // 128
                m.pres[i, j, h] = known[at % 128 : at % 128 + m.q, col : col + 1]

    for m in (small, big):

        def clear(c, carry):
            m.x2[c, pl.ds(0, m.half)] = jnp.zeros((m.half, H), BF)
            m.x2[c, pl.ds(5 * m.half, m.half)] = jnp.zeros((m.half, H), BF)

            @pl.when(g == 0)
            def _():
                m.x1[c, pl.ds(0, 2 * m.q)] = jnp.zeros((2 * m.q, H), BF)

            @pl.when(g == 7)
            def _():
                m.x1[c, pl.ds(10 * m.q, 2 * m.q)] = jnp.zeros((2 * m.q, H), BF)

            return carry

        lax.fori_loop(0, m.count if m is small else BIG, clear, 0)

    early = order[:2]
    lower_first(*early[0])
    weights["k0"].start()
    fetch(order[2:4])
    for name in ("out0", "in1"):
        weights[name].start()
    fetch(order[4:])
    for name in ("k1", "out1"):
        weights[name].start()
    lower_first(*early[1])
    pl.semaphore_wait(barrier, 5 + (g + 6) // 7 + (13 - g) // 7)
    for m, c in early:
        send_first(m, c)

    def at(p, stage):
        if stage is lower_first:
            p = p + jnp.where(p < 2, CHUNKS, 0)

        def short():
            run(small, p - BIG * (p >= FRONT).astype(jnp.int32))

        def run(m, c):
            stage(m, c)
            if stage is lower_first:
                send_first(m, c)

        if BIG:
            in_front = jnp.logical_and(p >= 0, p < FRONT)
            in_back = jnp.logical_and(p >= FRONT + BIG, p < CHUNKS)
            pl.when(jnp.logical_or(in_front, in_back))(short)
            pl.when(jnp.logical_and(p >= FRONT, p < FRONT + BIG))(lambda: run(big, p - FRONT))
        else:
            pl.when(jnp.logical_and(p >= 0, p < CHUNKS))(short)

    PLAN = [
        (near, 3),
        (pass_on, 5),
        (middle, 4),
        (far, 6),
        (lower_first, 0),
        (finish, 7),
        (send_halo, 1),
    ]

    def step(t, carry):
        for stage, lag in PLAN:
            at(t - lag, stage)
        return carry

    lax.fori_loop(0, CHUNKS + max(lag for _, lag in PLAN), step, 0)

    for m in (small, big):

        def drain(m, c):
            pl.when(g < 7)(lambda: halo_up(m, c).wait_send())
            pl.when(g > 0)(lambda: halo_down(m, c).wait_send())
            to_partner(m, c).wait_send()
            to_cross(m, c).wait_send()
            relay(m, c).wait_send()
            to_home(m, c).wait_send()

        lax.fori_loop(0, m.count if m is small else BIG, lambda c, carry: (drain(m, c), carry)[1], 0)


def body(stream, bases, input_weight, kernel_weight, output_weight):
    hbm = pl.BlockSpec(memory_space=pl.ANY)
    vmem = pl.BlockSpec(memory_space=pltpu.VMEM)
    shape = (2, PITCH // 32, 32, D)
    result = pl.pallas_call(
        kernel,
        out_shape=pltpu.VMEM(shape, BF),
        in_specs=[hbm, vmem, hbm, hbm, hbm],
        out_specs=vmem,
        scratch_shapes=[
            pltpu.VMEM((2, D, H), BF),
            pltpu.VMEM((2, TAPS * H, H), BF),
            pltpu.VMEM((2, H, D), BF),
            pltpu.SemaphoreType.DMA((6,)),
            *[ref for q, count in SETS for ref in Chunks(q, count, None).scratch()],
        ],
        compiler_params=pltpu.CompilerParams(
            collective_id=0, has_side_effects=True, vmem_limit_bytes=VMEM_LIMIT
        ),
    )(
        stream.reshape(shape),
        bases.reshape(14, 128),
        input_weight,
        kernel_weight.reshape(2, TAPS * H, H),
        output_weight,
    )
    return result.reshape(2 * PITCH, D)


def solution(mesh):
    return jax.shard_map(
        body,
        mesh=mesh,
        in_specs=(P(("batch", "seq"), None), P(("batch", "seq")), P(), P(), P()),
        out_specs=P(("batch", "seq"), None),
        check_vma=False,
    )
```

```python
import jax
import jax.numpy as jnp
from jax import lax
from jax.experimental import pallas as pl
from jax.experimental.pallas import tpu as pltpu
from jax.sharding import PartitionSpec as P

D, H, TAPS = 1280, 640, 5
PITCH = 896
FRONT, BIG, BACK = 1, 6, 1
CHUNKS = FRONT + BIG + BACK
BF, F32 = jnp.bfloat16, jnp.float32
PARTS = 2
VMEM_LIMIT = 54 * 2**20


def gelu_of_norm(v, mask=None):
    centre = v - jnp.mean(v, axis=-1, keepdims=True)
    scale = lax.rsqrt(jnp.mean(centre * centre, axis=-1, keepdims=True) + 1e-05)
    if mask is not None:
        scale = scale * mask
    u = centre * scale
    half = 0.5 * u
    bent = u * (0.7978845608028654 + 0.035677408136300125 * (u * u))
    return (half + half * jnp.tanh(bent)).astype(BF)


def dot(a, b):
    return jnp.dot(a, b, preferred_element_type=F32)


class Chunks:
    def __init__(self, q, count, refs):
        self.q, self.count = q, count
        self.rows, self.half = 8 * q, 4 * q
        count = PARTS if q == 32 else 1
        size = self.rows // count
        self.parts = [slice(i * size, (i + 1) * size) for i in range(count)]
        if refs is None:
            return
        (
            self.sbuf, self.resid, self.pres, self.s1, self.x1, self.s2, self.a1, self.x2,
            self.load_sem, self.a_s, self.a_r, self.h_s, self.h_r,
            self.b_s, self.b_r, self.y_s, self.y_r,
        ) = refs

    def scratch(self):
        q, n = self.q, self.count
        dma = pltpu.SemaphoreType.DMA
        plain = pltpu.VMEM((n, self.rows, H), BF)
        return [
            pltpu.VMEM((n, 4, 2, q, D), BF),
            pltpu.VMEM((n, self.rows, D), F32),
            pltpu.VMEM((n, 4, 2, q, 1), F32),
            plain,
            pltpu.VMEM((n, 12 * q, H), BF),
            plain,
            plain,
            pltpu.VMEM((n, 6 * self.half, H), BF),
            dma((n, 8)),
            dma((n, 3)),
            dma((n, 3)),
            dma((n, 2)),
            dma((n, 2)),
            dma((n, 3)),
            dma((n, 3)),
            dma((n, 4)),
            dma((n, 4)),
        ]


SETS = ((16, FRONT + BACK), (32, max(BIG, 1)))
FIELDS = 17


def rows(start, size):
    return pl.ds(pl.multiple_of(start, 16), size)


def kernel(x_hbm, bases, win_hbm, kern_hbm, wout_hbm, out, win, kern, wout, w_sem, *refs):
    small = Chunks(*SETS[0], refs[:FIELDS])
    big = Chunks(*SETS[1], refs[FIELDS:])
    s = lax.axis_index("seq")
    y, g, z = s // 8, s // 4, s % 4
    low = y % 2
    upper = y // 2
    own_v = low + upper - 2 * low * upper
    partner = s + 8 - 16 * low
    cross = (3 - y) * 8 + s % 8
    batch = lax.axis_index("batch")
    peers = [(z + k) % 4 for k in range(4)]
    ring = [s - z + p for p in peers]
    own_slot, partner_slot = y + 1, y + 2 - 2 * low
    keep, give = 1 - own_v, own_v

    def remote(src, dst, send, recv, dev):
        return pltpu.make_async_remote_copy(
            src_ref=src, dst_ref=dst, send_sem=send, recv_sem=recv,
            device_id=(dev, batch), device_id_type=pl.DeviceIdType.MESH,
        )

    def gather(m, c, k):
        p, n = peers[k], 2 * m.q
        return remote(
            m.s1.at[c, rows(p * n, n)], m.x1.at[c, rows((1 + z) * n, n)],
            m.a_s.at[c, k - 1], m.a_r.at[c, k - 1], ring[k],
        )

    def back(m, c, k):
        p, n = peers[k], 2 * m.q
        return remote(
            m.s2.at[c, rows(p * n, n)], m.a1.at[c, rows(z * n, n)],
            m.b_s.at[c, k - 1], m.b_r.at[c, k - 1], ring[k],
        )

    def halo_up(m, c):
        n = 2 * m.q
        return remote(
            m.x1.at[c, pl.ds(4 * n, n)], m.x1.at[c, pl.ds(0, n)],
            m.h_s.at[c, 0], m.h_r.at[c, 0], s + 4,
        )

    def halo_down(m, c):
        n = 2 * m.q
        return remote(
            m.x1.at[c, pl.ds(n, n)], m.x1.at[c, pl.ds(5 * n, n)],
            m.h_s.at[c, 1], m.h_r.at[c, 1], s - 4,
        )

    def to_partner(m, c):
        return remote(
            m.s2.at[c, rows(give * m.half, m.half)], m.x2.at[c, rows(own_slot * m.half, m.half)],
            m.y_s.at[c, 0], m.y_r.at[c, 0], partner,
        )

    def to_cross(m, c):
        return remote(
            m.s2.at[c, rows(keep * m.half, m.half)], m.x2.at[c, rows(own_slot * m.half, m.half)],
            m.y_s.at[c, 1], m.y_r.at[c, 1], cross,
        )

    def relay(m, c):
        part = m.x2.at[c, rows(partner_slot * m.half, m.half)]
        return remote(part, part, m.y_s.at[c, 2], m.y_r.at[c, 2], cross)

    def to_home(m, c):
        return remote(
            m.s1.at[c, rows((1 - low) * m.half, m.half)], m.a1.at[c, rows(keep * m.half, m.half)],
            m.y_s.at[c, 3], m.y_r.at[c, 3], partner,
        )

    def places(m, c):
        for h in range(2):
            if m is big:
                yield (h, pl.ds(2 * FRONT + 4 * c, 4)), (slice(None), h)
            else:
                behind = int(c >= FRONT) if isinstance(c, int) else (c >= FRONT).astype(jnp.int32)
                for i in range(4):
                    group = 2 * c + 4 * BIG * behind + i // 2
                    yield (h, group, pl.ds(16 * (i % 2), 16)), (i, h)

    def loads(m, c):
        return [
            pltpu.make_async_copy(x_hbm.at[there], m.sbuf.at[(c, *here)], m.load_sem.at[c, i])
            for i, (there, here) in enumerate(places(m, c))
        ]

    weights = {
        "in0": pltpu.make_async_copy(win_hbm.at[0], win.at[0], w_sem.at[0]),
        "k0": pltpu.make_async_copy(kern_hbm.at[0], kern.at[0], w_sem.at[1]),
        "out0": pltpu.make_async_copy(wout_hbm.at[0], wout.at[0], w_sem.at[2]),
        "in1": pltpu.make_async_copy(win_hbm.at[1], win.at[1], w_sem.at[3]),
        "k1": pltpu.make_async_copy(kern_hbm.at[1], kern.at[1], w_sem.at[4]),
        "out1": pltpu.make_async_copy(wout_hbm.at[1], wout.at[1], w_sem.at[5]),
    }

    def first(m, c, *names):
        if m is small:

            @pl.when(c == 0)
            def _():
                for name in names:
                    weights[name].wait()

    def lower_first(m, c):
        for copy in loads(m, c):
            copy.wait()
        if isinstance(c, int):
            first(m, c, "in0")
        mask = m.pres[c].reshape(m.rows, 1)
        v = m.sbuf[c].reshape(m.rows, D)
        normed = [gelu_of_norm(v[part].astype(F32)) for part in m.parts]
        lowered = [dot(n, win[0]) for n in normed]
        for part, low_part in zip(m.parts, lowered):
            m.s1[c, part] = gelu_of_norm(low_part, mask[part])

    def send_first(m, c):
        for k in (2, 1, 3):
            gather(m, c, k).start()
        n = 2 * m.q
        m.x1[c, rows((1 + z) * n, n)] = m.s1[c, rows(z * n, n)]

    def send_halo(m, c):
        for k in (1, 2, 3):
            gather(m, c, k).wait_recv()
        pl.when(g < 7)(lambda: halo_up(m, c).start())
        pl.when(g > 0)(lambda: halo_down(m, c).start())

    def near(m, c):
        first(m, c, "k0")
        pl.when(g > 0)(lambda: halo_up(m, c).wait_recv())
        pl.when(g < 7)(lambda: halo_down(m, c).wait_recv())
        for part in m.parts:
            size = part.stop - part.start
            wide = [m.x1[c, pl.ds(k * m.q + part.start, size)] for k in range(TAPS)]
            m.s2[c, part] = gelu_of_norm(dot(jnp.concatenate(wide, axis=1), kern[0]))
        for k in (2, 1, 3):
            back(m, c, k).start()
        n = 2 * m.q
        m.a1[c, rows(z * n, n)] = m.s2[c, rows(z * n, n)]

    def middle(m, c):
        first(m, c, "out0", "in1")
        for k in (1, 2, 3):
            back(m, c, k).wait_recv()
        for k in (1, 2, 3):
            back(m, c, k).wait_send()
        mask = m.pres[c].reshape(m.rows, 1)
        v = m.sbuf[c].reshape(m.rows, D)
        normed = []
        for part in m.parts:
            total = v[part].astype(F32) + dot(m.a1[c, part], wout[0])
            m.resid[c, part] = total
            normed.append(gelu_of_norm(total))
        lowered = [dot(n, win[1]) for n in normed]
        for part, low_part in zip(m.parts, lowered):
            m.s2[c, part] = gelu_of_norm(low_part, mask[part])
        to_partner(m, c).start()
        to_cross(m, c).start()
        m.x2[c, rows(own_slot * m.half, m.half)] = m.s2[c, rows(keep * m.half, m.half)]

    def pass_on(m, c):
        to_partner(m, c).wait_recv()
        relay(m, c).start()

    def far(m, c):
        first(m, c, "k1")
        to_cross(m, c).wait_recv()
        relay(m, c).wait_recv()
        for k in (1, 2, 3):
            gather(m, c, k).wait_send()
        for part in m.parts:
            size = part.stop - part.start
            wide = [m.x2[c, rows((upper + k) * m.half + part.start, size)] for k in range(4)]
            wide = jnp.concatenate(wide, axis=1)
            m.s1[c, part] = gelu_of_norm(dot(wide, kern[1, rows((1 - upper) * H, 4 * H)]))
        to_home(m, c).start()
        m.a1[c, rows(keep * m.half, m.half)] = m.s1[c, rows(low * m.half, m.half)]

    def finish(m, c):
        first(m, c, "out1")
        to_home(m, c).wait_recv()
        result = m.resid[c] + dot(m.a1[c], wout[1])
        result = result.astype(BF).reshape(4, 2, m.q, D)
        for there, here in places(m, c):
            out[there] = result[here]

    barrier = pltpu.get_barrier_semaphore()

    def greet(dev):
        pl.semaphore_signal(barrier, inc=1, device_id=(dev, batch), device_id_type=pl.DeviceIdType.MESH)

    for k in (1, 2, 3):
        greet(ring[k])
    greet(partner)
    greet(cross)
    pl.when(g < 7)(lambda: greet(s + 4))
    pl.when(g > 0)(lambda: greet(s - 4))

    order = [(small, c) for c in range(FRONT)]
    order += [(big, c) for c in range(BIG)]
    order += [(small, c) for c in range(FRONT, FRONT + BACK)]
    def fetch(some):
        for m, c in some:
            for copy in loads(m, c):
                copy.start()

    fetch(order[:1])
    weights["in0"].start()
    fetch(order[1:2])

    known = (bases[...] != 4).astype(F32).T
    for c, (m, i) in enumerate(order):
        n = 4 * m.q
        start = 64 * c if c <= FRONT else 64 * FRONT + 128 * (c - FRONT)
        if c > FRONT + BIG:
            start = 64 * (c - BIG) + 128 * BIG
        for h in range(2):
            for j in range(4):
                at = start + j * m.q
                col = h * 7 + at // 128
                m.pres[i, j, h] = known[at % 128 : at % 128 + m.q, col : col + 1]

    for m in (small, big):

        def clear(c, carry):
            m.x2[c, pl.ds(0, m.half)] = jnp.zeros((m.half, H), BF)
            m.x2[c, pl.ds(5 * m.half, m.half)] = jnp.zeros((m.half, H), BF)

            @pl.when(g == 0)
            def _():
                m.x1[c, pl.ds(0, 2 * m.q)] = jnp.zeros((2 * m.q, H), BF)

            @pl.when(g == 7)
            def _():
                m.x1[c, pl.ds(10 * m.q, 2 * m.q)] = jnp.zeros((2 * m.q, H), BF)

            return carry

        lax.fori_loop(0, m.count if m is small else BIG, clear, 0)

    early = order[:2]
    lower_first(*early[0])
    weights["k0"].start()
    fetch(order[2:4])
    for name in ("out0", "in1"):
        weights[name].start()
    fetch(order[4:])
    for name in ("k1", "out1"):
        weights[name].start()
    lower_first(*early[1])
    pl.semaphore_wait(barrier, 5 + (g + 6) // 7 + (13 - g) // 7)
    for m, c in early:
        send_first(m, c)

    def at(p, stage):
        if stage is lower_first:
            p = p + jnp.where(p < 2, CHUNKS, 0)

        def short():
            run(small, p - BIG * (p >= FRONT).astype(jnp.int32))

        def run(m, c):
            stage(m, c)
            if stage is lower_first:
                send_first(m, c)

        if BIG:
            in_front = jnp.logical_and(p >= 0, p < FRONT)
            in_back = jnp.logical_and(p >= FRONT + BIG, p < CHUNKS)
            pl.when(jnp.logical_or(in_front, in_back))(short)
            pl.when(jnp.logical_and(p >= FRONT, p < FRONT + BIG))(lambda: run(big, p - FRONT))
        else:
            pl.when(jnp.logical_and(p >= 0, p < CHUNKS))(short)

    PLAN = [
        (finish, 8),
        (near, 3),
        (pass_on, 5),
        (middle, 4),
        (far, 6),
        (lower_first, 0),
        (send_halo, 1),
    ]

    def step(t, carry):
        for stage, lag in PLAN:
            at(t - lag, stage)
        return carry

    lax.fori_loop(0, CHUNKS + max(lag for _, lag in PLAN), step, 0)

    for m in (small, big):

        def drain(m, c):
            pl.when(g < 7)(lambda: halo_up(m, c).wait_send())
            pl.when(g > 0)(lambda: halo_down(m, c).wait_send())
            to_partner(m, c).wait_send()
            to_cross(m, c).wait_send()
            relay(m, c).wait_send()
            to_home(m, c).wait_send()

        lax.fori_loop(0, m.count if m is small else BIG, lambda c, carry: (drain(m, c), carry)[1], 0)


def body(stream, bases, input_weight, kernel_weight, output_weight):
    hbm = pl.BlockSpec(memory_space=pl.ANY)
    vmem = pl.BlockSpec(memory_space=pltpu.VMEM)
    shape = (2, PITCH // 32, 32, D)
    result = pl.pallas_call(
        kernel,
        out_shape=pltpu.VMEM(shape, BF),
        in_specs=[hbm, vmem, hbm, hbm, hbm],
        out_specs=vmem,
        scratch_shapes=[
            pltpu.VMEM((2, D, H), BF),
            pltpu.VMEM((2, TAPS * H, H), BF),
            pltpu.VMEM((2, H, D), BF),
            pltpu.SemaphoreType.DMA((6,)),
            *[ref for q, count in SETS for ref in Chunks(q, count, None).scratch()],
        ],
        compiler_params=pltpu.CompilerParams(
            collective_id=0, has_side_effects=True, vmem_limit_bytes=VMEM_LIMIT
        ),
    )(
        stream.reshape(shape),
        bases.reshape(14, 128),
        input_weight,
        kernel_weight.reshape(2, TAPS * H, H),
        output_weight,
    )
    return result.reshape(2 * PITCH, D)


def solution(mesh):
    return jax.shard_map(
        body,
        mesh=mesh,
        in_specs=(P(("batch", "seq"), None), P(("batch", "seq")), P(), P(), P()),
        out_specs=P(("batch", "seq"), None),
        check_vma=False,
    )
```
